128 devices in a mesh: grp: 128 (over z, y, x, core).
Axes of the slice: x: 4, y: 4, z: 4, core: 2. Of those that a mesh axis runs over, the one named last changes fastest.
Arguments:
- right_side: float32 [384, 256, 2048], P('grp'), may hold values from -12 to 12
- fine_smoother: float32 [1, 256, 256], replicated, may hold values from -0.1 to 0.1
- level_two_smoother: float32 [128, 128], replicated, may hold values from -0.25 to 0.25
- level_three_smoother: float32 [64, 64], replicated, may hold values from -0.25 to 0.25
- level_four_smoother: float32 [32, 32], replicated, may hold values from -0.25 to 0.25
Outputs:
- solution: float32 [384, 256, 2048], P('grp')
- pending_correction: float32 [384, 256, 2048], P('grp')
The draws below stay inside these ranges and needn't reach their ends.
All inputs are finite; a program needn't handle non-finite values.
Results may differ from the reference program's by a relative error of at most 0.0003.
Values sent between devices are 32-bit elements; how exact they have to be, the bound alone decides.
A program may use at most 192 MiB of HBM per device.

```python
import jax
import jax.numpy as jnp
from jax import lax

NZ = 256
BZ = 256
NY = 2048
NX = 384


def smoother_entries(key, leading, order, lowest, highest):
    diag_key, off_key = jax.random.split(key)
    diagonal = jax.random.uniform(diag_key, leading + (order,), jnp.float32, lowest, highest)
    spread = 0.3 * 0.5 * (lowest + highest) / order ** 0.5
    off_diag = spread * jax.random.truncated_normal(off_key, -3.0, 3.0, leading + (order, order), jnp.float32)
    identity = jnp.eye(order, dtype=jnp.float32)
    return diagonal[..., :, None] * identity + off_diag * (1.0 - identity)


def draw_fine_smoother(key, part):
    key = jax.random.fold_in(key, 11)
    return smoother_entries(key, (NZ // BZ,), BZ, 0.05, 0.1)


def draw_level_two_smoother(key, part):
    key = jax.random.fold_in(key, 12)
    return smoother_entries(key, (), NZ // 2, 0.1, 0.25)


def draw_level_three_smoother(key, part):
    key = jax.random.fold_in(key, 13)
    return smoother_entries(key, (), NZ // 4, 0.1, 0.25)


def draw_level_four_smoother(key, part):
    key = jax.random.fold_in(key, 14)
    return smoother_entries(key, (), NZ // 8, 0.1, 0.25)


def level_of(stream_key, shape, pieces, least, top_value):
    factor_of = 1.0
    for dim, parts in pieces:
        steps = jax.random.uniform(jax.random.fold_in(jax.random.fold_in(stream_key, 6), dim), (parts,), jnp.float32, least / len(pieces), top_value / len(pieces))
        factor_of = factor_of * jnp.repeat(jnp.exp(steps), shape[dim] // parts).reshape((-1,) + (1,) * (len(shape) - 1 - dim))
    return factor_of


def gaussian(stream_key, extent, deviation, most, pieces=(), held_as=jnp.bfloat16):
    gain = level_of(stream_key, extent, pieces, -0.22, 0.18) if pieces else 1.0
    values = jax.random.normal(stream_key, extent, jnp.float32) * deviation * gain
    return jnp.minimum(jnp.maximum(values, -most), most).astype(held_as)


def setup_inputs(seed: int = 0) -> dict:
    key_of = jax.random.split(jax.random.key(seed), 6)
    return {
        "right_side": gaussian(key_of[0], (NX, NZ, NY), 2.0, 12.0, ((0, 128),), jnp.float32),
        "fine_smoother": draw_fine_smoother(jax.random.fold_in(key_of[5], 71), 0),
        "level_two_smoother": draw_level_two_smoother(jax.random.fold_in(key_of[5], 71), 0),
        "level_three_smoother": draw_level_three_smoother(jax.random.fold_in(key_of[5], 71), 0),
        "level_four_smoother": draw_level_four_smoother(jax.random.fold_in(key_of[5], 71), 0),
    }


FINE_Z = 4.0


def line_apply(matrix, source):
    if matrix.ndim == 2:
        matrix = matrix[None]
    block_count, block_size, _ = matrix.shape
    planes, layers, span_y = source.shape
    blocked = source.reshape(planes, block_count, block_size, span_y)
    result = jnp.einsum("bij,xbjy->xbiy", matrix, blocked, precision=lax.Precision.HIGHEST)
    return result.reshape(planes, layers, span_y)


def operate(extended, vertical):
    centre = extended[1:-1]
    beside_x = extended[2:] + extended[:-2]
    padded_z = jnp.pad(centre, ((0, 0), (1, 1), (0, 0)))
    beside_z = padded_z[:, 2:] + padded_z[:, :-2]
    padded_y = jnp.pad(centre, ((0, 0), (0, 0), (1, 1)))
    beside_y = padded_y[:, :, 2:] + padded_y[:, :, :-2]
    return (2.0 * centre - beside_x) + (2.0 * centre - beside_y) + vertical * (2.0 * centre - beside_z)


def pad_planes(source):
    return jnp.pad(source, ((1, 1), (0, 0), (0, 0)))


def restrict(source, factor):
    planes, layers, span_y = source.shape
    return source.reshape(planes, layers // factor, factor, span_y).sum(axis=2)


def smooth(matrix, source, vertical):
    first_pass = line_apply(matrix, source)
    return first_pass + line_apply(matrix, source - operate(pad_planes(first_pass), vertical))


def coarse_pass(matrices, source):
    summed = jnp.zeros_like(source)
    for matrix, factor, vertical in zip(matrices, (2, 4, 8), (FINE_Z / 4.0, FINE_Z / 16.0, FINE_Z / 64.0)):
        smoothed = smooth(matrix, restrict(source, factor), vertical)
        summed = summed + jnp.repeat(smoothed, factor, axis=1)
    return summed


def reference(right_side, fine_smoother, level_two_smoother, level_three_smoother, level_four_smoother):
    matrices = (level_two_smoother, level_three_smoother, level_four_smoother)
    first_iterate = smooth(fine_smoother, right_side, FINE_Z)
    residual = right_side - operate(pad_planes(first_iterate), FINE_Z)
    solution = first_iterate + smooth(fine_smoother, residual, FINE_Z) + coarse_pass(matrices, right_side)
    pending_correction = coarse_pass(matrices, residual)
    return solution, pending_correction
```

```python
import jax
import jax.numpy as jnp
from jax import lax
from jax.experimental import pallas as pl
from jax.experimental.pallas import tpu as pltpu
from jax.sharding import PartitionSpec as P

MESH = pl.DeviceIdType.MESH
F32 = jnp.float32
BF16 = jnp.bfloat16

FINE_Z = 4.0
LANES = 128
AHEAD = 3
LAG = 4
ROWS = 64


def parts_of(m):
    head = m.astype(BF16)
    rest = m - head.astype(F32)
    middle = rest.astype(BF16)
    return head, middle, (rest - middle.astype(F32)).astype(BF16)


def exact_dot(a, b):
    a1, a2, a3 = parts_of(a)
    b1, b2, b3 = parts_of(b)
    left = jnp.concatenate([a1, a1, a2, a1, a2, a3], axis=1)
    right = jnp.concatenate([b1, b2, b1, b3, b2, b1], axis=0)
    return jnp.dot(left, right, preferred_element_type=F32)


def second_difference(m):
    order = m.shape[0]
    row = lax.broadcasted_iota(jnp.int32, m.shape, 0)
    below = jnp.where(row == 0, 0.0, pltpu.roll(m, 1, 0))
    above = jnp.where(row == order - 1, 0.0, pltpu.roll(m, order - 1, 0))
    return 2.0 * m - below - above


def line_pair(m, vertical):
    square = exact_dot(m, m)
    mixed = exact_dot(m, second_difference(m))
    return 2.0 * m - vertical * mixed - 4.0 * square, square


def spread(rows, columns, factor):
    row = lax.broadcasted_iota(jnp.int32, (rows, columns), 0)
    column = lax.broadcasted_iota(jnp.int32, (rows, columns), 1)
    return ((row >= factor * column) & (row < factor * column + factor)).astype(F32)


def gather(rows, columns, factor):
    row = lax.broadcasted_iota(jnp.int32, (rows, columns), 0)
    column = lax.broadcasted_iota(jnp.int32, (rows, columns), 1)
    return ((column >= factor * row) & (column < factor * row + factor)).astype(F32)


def build_terms(fine, two, three, four, coarse, left_terms, right_terms, product, totals, doubled, terms):
    nz = fine.shape[0]
    half = nz // 2
    p0, q = line_pair(fine, FINE_Z)

    def scaled(m):
        return 4.0 * m + FINE_Z * second_difference(m)

    row = lax.broadcasted_iota(jnp.int32, (nz, nz), 0)
    column = lax.broadcasted_iota(jnp.int32, (nz, nz), 1)
    left_terms[0:nz] = p0
    left_terms[nz : 2 * nz] = q
    right_terms[0] = (row == column).astype(F32) - scaled(p0)
    right_terms[1] = p0 - scaled(q)
    right_terms[2] = q

    c0, c1 = line_pair(two, FINE_Z / 4.0)
    for m, factor, vertical in ((three, 2, FINE_Z / 16.0), (four, 4, FINE_Z / 64.0)):
        up, down = spread(half, half, factor), gather(half, half, factor)
        wide = exact_dot(up, jnp.concatenate(line_pair(m, vertical), axis=1))
        coarse[0:half] = wide[:, 0:half]
        coarse[half:nz] = wide[:, half:nz]
        both = exact_dot(coarse[...], down)
        c0 = c0 + both[0:half]
        c1 = c1 + both[half:nz]
    coarse[0:half] = c0
    coarse[half:nz] = c1
    both = exact_dot(coarse[...], gather(half, nz, 2))
    left_terms[2 * nz : 3 * nz] = both
    for k, base in ((0, p0), (1, q)):
        for h in range(nz // LANES):
            columns = slice(h * LANES, (h + 1) * LANES)
            part = left_terms[2 * nz + k * half : 2 * nz + (k + 1) * half, columns]
            for side in range(2):
                doubled[h, pl.ds(side, half, stride=2)] = part
            totals[k, 0:nz, columns] = base[:, columns] + doubled[h]
    for k in range(4):
        if k >= 2:
            totals[k, 0:nz] = jnp.zeros((nz, nz), F32)
        totals[k, nz : nz + half] = jnp.zeros((half, nz), F32)
    for j in range(3):
        product[...] = exact_dot(left_terms[...], right_terms[j])
        totals[j, 0:nz] += product[0:nz]
        totals[j + 1, 0:nz] += product[nz : 2 * nz]
        totals[j, nz : nz + half] += product[2 * nz : 2 * nz + half]
        totals[j + 1, nz : nz + half] += product[2 * nz + half : 3 * nz]
    for k in range(4):
        total = totals[k]
        head = total.astype(BF16)
        terms[k, :, 0:nz] = head
        terms[k, :, nz : 2 * nz] = head
        terms[k, :, 2 * nz : 3 * nz] = (total - head.astype(F32)).astype(BF16)


def stacked(planes):
    cells = jnp.concatenate(planes, axis=1)
    head = cells.astype(BF16)
    tail = (cells - head.astype(F32)).astype(BF16)
    return jnp.concatenate([head, tail, head], axis=0)


def kernel(
    count,
    right_side, fine, two, three, four,
    sol, pend,
    own, near_l, near_r, far_l, far_r,
    v3, v2, v1, v0,
    fine_v, two_v, three_v, four_v, left_terms, right_terms, product, totals, terms, doubled, padded, coarse,
    own_sem, small_sem, near_send, near_recv, far_send, far_recv,
):
    me = lax.axis_index("grp")
    has_l, has_r = me > 0, me < count - 1
    chunks = own.shape[0]
    rows = v0.shape[2]
    nz = own.shape[2]

    barrier = pltpu.get_barrier_semaphore()

    @pl.when(has_l)
    def _():
        pl.semaphore_signal(barrier, inc=1, device_id=(me - 1,), device_id_type=MESH)

    @pl.when(has_r)
    def _():
        pl.semaphore_signal(barrier, inc=1, device_id=(me + 1,), device_id_type=MESH)

    pl.semaphore_wait(barrier, has_l.astype(jnp.int32) + has_r.astype(jnp.int32))

    def cut(c):
        return pl.ds(pl.multiple_of(c * LANES, LANES), LANES)

    def remote(planes, buffer, sends, recvs, way, c, target):
        return pltpu.make_async_remote_copy(
            src_ref=right_side.at[planes, :, cut(c)],
            dst_ref=buffer.at[c],
            send_sem=sends.at[way, c],
            recv_sem=recvs.at[way, c],
            device_id=(target,),
            device_id_type=MESH,
        )

    def near_left(c):
        return remote(pl.ds(0, 2), near_r, near_send, near_recv, 0, c, me - 1)

    def near_right(c):
        return remote(pl.ds(1, 2), near_l, near_send, near_recv, 1, c, me + 1)

    def far_left(c):
        return remote(2, far_r, far_send, far_recv, 0, c, me - 1)

    def far_right(c):
        return remote(0, far_l, far_send, far_recv, 1, c, me + 1)

    def start(to_left, to_right, c):
        @pl.when(has_l)
        def _():
            to_left(c).start()

        @pl.when(has_r)
        def _():
            to_right(c).start()

    def finish(to_left, to_right, c):
        @pl.when(has_l)
        def _():
            to_left(c).wait_send()
            to_right(c).wait_recv()

        @pl.when(has_r)
        def _():
            to_right(c).wait_send()
            to_left(c).wait_recv()

    for c in range(AHEAD):
        start(near_left, near_right, c)

    small = [
        pltpu.make_async_copy(src, dst, small_sem.at[i])
        for i, (src, dst) in enumerate(
            ((fine.at[0], fine_v), (two, two_v), (three, three_v), (four, four_v))
        )
    ]
    for copy in small:
        copy.start()

    def own_copy(c):
        return pltpu.make_async_copy(right_side.at[:, :, cut(c)], own.at[c], own_sem.at[c])

    lax.fori_loop(0, chunks, lambda c, _: (own_copy(c).start(), 0)[1], 0)

    plane = jnp.zeros((rows, LANES), F32)
    for ring in (v3, v2, v1):
        for p in range(ring.shape[1]):
            ring[ring.shape[0] - 1, p] = plane
    for slot in range(v3.shape[0]):
        v3[slot, 0] = plane
        v3[slot, v3.shape[1] - 1] = plane

    def clear(near, far):
        def body(c, _):
            near[c] = jnp.zeros(near.shape[1:], F32)
            far[c] = jnp.zeros(far.shape[1:], F32)
            return 0

        lax.fori_loop(0, chunks, body, 0)

    @pl.when(jnp.logical_not(has_l))
    def _():
        clear(near_l, far_l)

    @pl.when(jnp.logical_not(has_r))
    def _():
        clear(near_r, far_r)

    for copy in small:
        copy.wait()
    for i, m in enumerate((three_v, four_v)):
        order = m.shape[0]
        padded[i] = jnp.zeros(padded.shape[1:], F32)
        padded[i, 0:order, 0:order] = m[...]
    build_terms(fine_v[...], two_v[...], padded[0], padded[1], coarse,
        left_terms, right_terms, product, totals, doubled, terms)

    def slot(ring, c):
        return lax.rem(c, ring.shape[0])

    def spread_out(c):
        s3, s2, s1, s0 = slot(v3, c), slot(v2, c), slot(v1, c), slot(v0, c)
        rings = {3: (v3, s3, 3), 2: (v2, s2, 2), 1: (v1, s1, 1), 0: (v0, s0, 0)}

        def apply(places, planes, orders):
            source = stacked(planes)
            for k in orders:
                ring, s, offset = rings[k]
                product = jnp.dot(terms[k], source, preferred_element_type=F32)
                for i, x in enumerate(places):
                    ring[s, x + offset] = product[:, i * LANES : (i + 1) * LANES]

        apply((0, 1, 2), [own[c, 0], own[c, 1], own[c, 2]], (3, 2, 1, 0))
        apply((-1, 3), [near_l[c, 1], near_r[c, 0]], (3, 2, 1))
        apply((-2, 4), [near_l[c, 0], near_r[c, 1]], (3, 2))

    lane = lax.broadcasted_iota(jnp.int32, (ROWS, LANES), 1)
    first_lane, last_lane = lane == 0, lane == LANES - 1

    def neighbours(source, target, shift, lo, hi, t):
        before, here, after = slot(source, t + source.shape[0] - 1), slot(source, t), slot(source, t + 1)
        into = slot(target, t)

        def body(p, _):
            q = p + shift
            for b in range(rows // ROWS):
                part = pl.ds(b * ROWS, ROWS)
                centre = source[here, q, part]
                up = pltpu.roll(jnp.where(first_lane, source[after, q, part], centre), LANES - 1, 1)
                down = pltpu.roll(jnp.where(last_lane, source[before, q, part], centre), 1, 1)
                beside = source[here, q - 1, part] + source[here, q + 1, part]
                target[into, p, part] = target[into, p, part] + (beside + (up + down))
            return 0

        lax.fori_loop(lo, hi, body, 0)

    skip_l = jnp.where(has_l, 0, 1)
    skip_r = jnp.where(has_r, 0, 1)

    def add_far(j):
        source = stacked([far_l[j], far_r[j]])
        product = jnp.dot(terms[3], source, preferred_element_type=F32)
        s = slot(v0, j)
        columns = cut(j)
        for p in range(3):
            total = v0[s, p]
            if p == 0:
                total = total + product[:, 0:LANES]
            if p == 2:
                total = total + product[:, LANES : 2 * LANES]
            sol[p, :, columns] = total[0:nz]
            for side in range(2):
                doubled[p, pl.ds(side, nz // 2, stride=2)] = total[nz:rows]
            pend[p, :, columns] = doubled[p]

    def zero_slot(ring, c):
        def body(p, _):
            ring[slot(ring, c), p] = jnp.zeros((rows, LANES), F32)
            return 0

        lax.fori_loop(0, ring.shape[1], body, 0)

    def step(c, _):
        @pl.when(c < chunks)
        def _():
            own_copy(c).wait()
            finish(near_left, near_right, c)

        @pl.when(c + AHEAD < chunks)
        def _():
            start(near_left, near_right, c + AHEAD)

            @pl.when(c + AHEAD >= LAG)
            def _():
                start(far_left, far_right, c + AHEAD - LAG)

        @pl.when(c + AHEAD == chunks)
        def _():
            for i in range(LAG):
                start(far_left, far_right, chunks - LAG + i)

        @pl.when(c < chunks)
        def _():
            spread_out(c)

        @pl.when(c == chunks)
        def _():
            zero_slot(v3, chunks)

        @pl.when((c >= 1) & (c < chunks + 1))
        def _():
            neighbours(v3, v2, 1, 2 * skip_l, 7 - 2 * skip_r, c - 1)

        @pl.when(c == chunks + 1)
        def _():
            zero_slot(v2, chunks)

        @pl.when((c >= 2) & (c < chunks + 2))
        def _():
            neighbours(v2, v1, 1, skip_l, 5 - skip_r, c - 2)

        @pl.when(c == chunks + 2)
        def _():
            zero_slot(v1, chunks)

        @pl.when((c >= 3) & (c < chunks + 3))
        def _():
            neighbours(v1, v0, 1, 0, 3, c - 3)

        @pl.when(c >= LAG)
        def _():
            finish(far_left, far_right, c - LAG)
            add_far(c - LAG)

        return 0

    lax.fori_loop(0, chunks + LAG, step, 0)


def put_out(sol, pend, sol_out, pend_out, sems):
    copies = []
    for p in range(sol.shape[0]):
        copies.append(pltpu.make_async_copy(sol.at[p], sol_out.at[p], sems.at[0, p]))
        copies.append(pltpu.make_async_copy(pend.at[p], pend_out.at[p], sems.at[1, p]))
    for copy in copies:
        copy.start()
    for copy in copies:
        copy.wait()


def solution(mesh):
    count = mesh.shape["grp"]
    anywhere = pl.BlockSpec(memory_space=pl.ANY)
    vmem = pl.BlockSpec(memory_space=pltpu.VMEM)

    def per_device(right_side, fine, two, three, four):
        planes, nz, ny = right_side.shape
        chunks = ny // LANES
        rows = nz + nz // 2
        shape = (planes, nz, ny)

        def body(*refs):
            kernel(count, *refs)

        sol, pend = pl.pallas_call(
            body,
            out_shape=(pltpu.VMEM(shape, F32), pltpu.VMEM(shape, F32)),
            in_specs=[anywhere] * 5,
            out_specs=(vmem, vmem),
            scratch_shapes=[
                pltpu.VMEM((chunks, planes, nz, LANES), F32),
                pltpu.VMEM((chunks, 2, nz, LANES), F32),
                pltpu.VMEM((chunks, 2, nz, LANES), F32),
                pltpu.VMEM((chunks, nz, LANES), F32),
                pltpu.VMEM((chunks, nz, LANES), F32),
                pltpu.VMEM((3, planes + 6, rows, LANES), F32),
                pltpu.VMEM((4, planes + 4, rows, LANES), F32),
                pltpu.VMEM((5, planes + 2, rows, LANES), F32),
                pltpu.VMEM((5, planes, rows, LANES), F32),
                pltpu.VMEM(fine.shape[1:], F32),
                pltpu.VMEM(two.shape, F32),
                pltpu.VMEM(three.shape, F32),
                pltpu.VMEM(four.shape, F32),
                pltpu.VMEM((3 * nz, nz), F32),
                pltpu.VMEM((3, nz, nz), F32),
                pltpu.VMEM((3 * nz, nz), F32),
                pltpu.VMEM((4, rows, nz), F32),
                pltpu.VMEM((4, rows, 3 * nz), BF16),
                pltpu.VMEM((planes, nz, LANES), F32),
                pltpu.VMEM((2, nz // 2, nz // 2), F32),
                pltpu.VMEM((nz, nz // 2), F32),
                pltpu.SemaphoreType.DMA((chunks,)),
                pltpu.SemaphoreType.DMA((4,)),
                pltpu.SemaphoreType.DMA((2, chunks)),
                pltpu.SemaphoreType.DMA((2, chunks)),
                pltpu.SemaphoreType.DMA((2, chunks)),
                pltpu.SemaphoreType.DMA((2, chunks)),
            ],
            compiler_params=pltpu.CompilerParams(
                collective_id=1, has_side_effects=True, vmem_limit_bytes=50 << 20
            ),
        )(right_side, fine, two, three, four)
        sol = pltpu.with_memory_space_constraint(sol, pltpu.VMEM)
        pend = pltpu.with_memory_space_constraint(pend, pltpu.VMEM)
        return pl.pallas_call(
            put_out,
            out_shape=(jax.ShapeDtypeStruct(shape, F32), jax.ShapeDtypeStruct(shape, F32)),
            in_specs=[vmem, vmem],
            out_specs=(anywhere, anywhere),
            scratch_shapes=[pltpu.SemaphoreType.DMA((2, planes))],
            compiler_params=pltpu.CompilerParams(vmem_limit_bytes=16 << 20),
        )(sol, pend)

    in_specs = (P("grp", None, None), P(), P(), P(), P())
    out_specs = (P("grp", None, None), P("grp", None, None))
    return jax.shard_map(
        per_device, mesh=mesh, in_specs=in_specs, out_specs=out_specs, check_vma=False
    )
```

```python
import jax
import jax.numpy as jnp
from jax import lax
from jax.experimental import pallas as pl
from jax.experimental.pallas import tpu as pltpu
from jax.sharding import PartitionSpec as P

MESH = pl.DeviceIdType.MESH
F32 = jnp.float32
BF16 = jnp.bfloat16

FINE_Z = 4.0
LANES = 128
AHEAD = 3
LAG = 6
ROWS = 32


def parts_of(m):
    head = m.astype(BF16)
    rest = m - head.astype(F32)
    middle = rest.astype(BF16)
    return head, middle, (rest - middle.astype(F32)).astype(BF16)


def exact_dot(a, b):
    a1, a2, a3 = parts_of(a)
    b1, b2, b3 = parts_of(b)
    left = jnp.concatenate([a1, a1, a2, a1, a2, a3], axis=1)
    right = jnp.concatenate([b1, b2, b1, b3, b2, b1], axis=0)
    return jnp.dot(left, right, preferred_element_type=F32)


def second_difference(m):
    order = m.shape[0]
    row = lax.broadcasted_iota(jnp.int32, m.shape, 0)
    below = jnp.where(row == 0, 0.0, pltpu.roll(m, 1, 0))
    above = jnp.where(row == order - 1, 0.0, pltpu.roll(m, order - 1, 0))
    return 2.0 * m - below - above


def line_pair(m, vertical):
    square = exact_dot(m, m)
    mixed = exact_dot(m, second_difference(m))
    return 2.0 * m - vertical * mixed - 4.0 * square, square


def spread(rows, columns, factor):
    row = lax.broadcasted_iota(jnp.int32, (rows, columns), 0)
    column = lax.broadcasted_iota(jnp.int32, (rows, columns), 1)
    return ((row >= factor * column) & (row < factor * column + factor)).astype(F32)


def gather(rows, columns, factor):
    row = lax.broadcasted_iota(jnp.int32, (rows, columns), 0)
    column = lax.broadcasted_iota(jnp.int32, (rows, columns), 1)
    return ((column >= factor * row) & (column < factor * row + factor)).astype(F32)


def build_terms(fine, two, three, four, coarse, left_terms, right_terms, product, totals, doubled, terms):
    nz = fine.shape[0]
    half = nz // 2
    p0, q = line_pair(fine, FINE_Z)

    def scaled(m):
        return 4.0 * m + FINE_Z * second_difference(m)

    row = lax.broadcasted_iota(jnp.int32, (nz, nz), 0)
    column = lax.broadcasted_iota(jnp.int32, (nz, nz), 1)
    left_terms[0:nz] = p0
    left_terms[nz : 2 * nz] = q
    right_terms[0] = (row == column).astype(F32) - scaled(p0)
    right_terms[1] = p0 - scaled(q)
    right_terms[2] = q

    c0, c1 = line_pair(two, FINE_Z / 4.0)
    for m, factor, vertical in ((three, 2, FINE_Z / 16.0), (four, 4, FINE_Z / 64.0)):
        up, down = spread(half, half, factor), gather(half, half, factor)
        wide = exact_dot(up, jnp.concatenate(line_pair(m, vertical), axis=1))
        coarse[0:half] = wide[:, 0:half]
        coarse[half:nz] = wide[:, half:nz]
        both = exact_dot(coarse[...], down)
        c0 = c0 + both[0:half]
        c1 = c1 + both[half:nz]
    coarse[0:half] = c0
    coarse[half:nz] = c1
    both = exact_dot(coarse[...], gather(half, nz, 2))
    left_terms[2 * nz : 3 * nz] = both
    for k, base in ((0, p0), (1, q)):
        for h in range(nz // LANES):
            columns = slice(h * LANES, (h + 1) * LANES)
            part = left_terms[2 * nz + k * half : 2 * nz + (k + 1) * half, columns]
            for side in range(2):
                doubled[h, pl.ds(side, half, stride=2)] = part
            totals[k, 0:nz, columns] = base[:, columns] + doubled[h]
    for k in range(4):
        if k >= 2:
            totals[k, 0:nz] = jnp.zeros((nz, nz), F32)
        totals[k, nz : nz + half] = jnp.zeros((half, nz), F32)
    for j in range(3):
        product[...] = exact_dot(left_terms[...], right_terms[j])
        totals[j, 0:nz] += product[0:nz]
        totals[j + 1, 0:nz] += product[nz : 2 * nz]
        totals[j, nz : nz + half] += product[2 * nz : 2 * nz + half]
        totals[j + 1, nz : nz + half] += product[2 * nz + half : 3 * nz]
    for k in range(4):
        total = totals[k]
        columns = slice(k * nz, (k + 1) * nz)
        head = total.astype(BF16)
        terms[0 : nz + half, columns] = head
        terms[nz + half :, columns] = (total - head.astype(F32)).astype(BF16)


def halves(cells):
    head = cells.astype(BF16)
    return head, (cells - head.astype(F32)).astype(BF16)


def product_of(terms, columns, head, tail):
    rows = terms.shape[0] // 2
    both = jnp.dot(terms[:, columns], head, preferred_element_type=F32)
    rest = jnp.dot(terms[0:rows, columns], tail, preferred_element_type=F32)
    return both[0:rows] + (both[rows:] + rest)


def kernel(
    count,
    right_side, fine, two, three, four,
    sol, pend,
    cells, far_l, far_r,
    once, twice, head, tail, sums,
    fine_v, two_v, three_v, four_v, left_terms, right_terms, product, totals, terms, doubled, padded, coarse,
    own_sem, small_sem, near_send, near_recv, far_send, far_recv,
):
    me = lax.axis_index("grp")
    has_l, has_r = me > 0, me < count - 1
    chunks = far_l.shape[0]
    rows = sums.shape[2]
    nz = cells.shape[2]

    barrier = pltpu.get_barrier_semaphore()

    @pl.when(has_l)
    def _():
        pl.semaphore_signal(barrier, inc=1, device_id=(me - 1,), device_id_type=MESH)

    @pl.when(has_r)
    def _():
        pl.semaphore_signal(barrier, inc=1, device_id=(me + 1,), device_id_type=MESH)

    pl.semaphore_wait(barrier, has_l.astype(jnp.int32) + has_r.astype(jnp.int32))

    def cut(c):
        return pl.ds(pl.multiple_of(c * LANES, LANES), LANES)

    def remote(planes, target, sends, recvs, way, c, device):
        return pltpu.make_async_remote_copy(
            src_ref=right_side.at[planes, :, cut(c)],
            dst_ref=target,
            send_sem=sends.at[way, c],
            recv_sem=recvs.at[way, c],
            device_id=(device,),
            device_id_type=MESH,
        )

    def near_left(c):
        target = cells.at[c + 1, pl.ds(5, 2)]
        return remote(pl.ds(0, 2), target, near_send, near_recv, 0, c, me - 1)

    def near_right(c):
        target = cells.at[c + 1, pl.ds(0, 2)]
        return remote(pl.ds(1, 2), target, near_send, near_recv, 1, c, me + 1)

    def far_left(c):
        return remote(2, far_r.at[c], far_send, far_recv, 0, c, me - 1)

    def far_right(c):
        return remote(0, far_l.at[c], far_send, far_recv, 1, c, me + 1)

    def start(to_left, to_right, c):
        @pl.when(has_l)
        def _():
            to_left(c).start()

        @pl.when(has_r)
        def _():
            to_right(c).start()

    def finish(to_left, to_right, c):
        @pl.when(has_l)
        def _():
            to_left(c).wait_send()
            to_right(c).wait_recv()

        @pl.when(has_r)
        def _():
            to_right(c).wait_send()
            to_left(c).wait_recv()

    for c in range(AHEAD):
        start(near_left, near_right, c)

    small = [
        pltpu.make_async_copy(src, dst, small_sem.at[i])
        for i, (src, dst) in enumerate(
            ((fine.at[0], fine_v), (two, two_v), (three, three_v), (four, four_v))
        )
    ]
    for copy in small:
        copy.start()

    def own_copy(c):
        return pltpu.make_async_copy(
            right_side.at[:, :, cut(c)], cells.at[c + 1, pl.ds(2, 3)], own_sem.at[c]
        )

    lax.fori_loop(0, chunks, lambda c, _: (own_copy(c).start(), 0)[1], 0)

    plane = jnp.zeros((nz, LANES), F32)
    for p in range(7):
        cells[0, p] = plane
        cells[chunks + 1, p] = plane

    def clear(ring, s, planes):
        for p in planes:
            ring[s, p] = plane

    clear(once, once.shape[0] - 1, range(7))
    clear(twice, twice.shape[0] - 1, range(5))

    @pl.when(jnp.logical_not(has_l))
    def _():
        def body(c, _):
            clear(cells, c + 1, range(0, 2))
            far_l[c] = plane
            return 0

        lax.fori_loop(0, chunks, body, 0)

    @pl.when(jnp.logical_not(has_r))
    def _():
        def body(c, _):
            clear(cells, c + 1, range(5, 7))
            far_r[c] = plane
            return 0

        lax.fori_loop(0, chunks, body, 0)

    for copy in small:
        copy.wait()
    for i, m in enumerate((three_v, four_v)):
        order = m.shape[0]
        padded[i] = jnp.zeros(padded.shape[1:], F32)
        padded[i, 0:order, 0:order] = m[...]
    build_terms(fine_v[...], two_v[...], padded[0], padded[1], coarse,
        left_terms, right_terms, product, totals, doubled, terms)

    def slot(ring, c):
        return lax.rem(c, ring.shape[0])

    lane = lax.broadcasted_iota(jnp.int32, (ROWS, LANES), 1)
    first_lane, last_lane = lane == 0, lane == LANES - 1

    def neighbour_sum(source, slots, targets, put):
        before, here, after = slots
        for b in range(nz // ROWS):
            part = pl.ds(b * ROWS, ROWS)
            centres = [source[here, q, part] for q in range(source.shape[1])]
            for p, q in targets:
                up = jnp.where(first_lane, source[after, q, part], centres[q])
                down = jnp.where(last_lane, source[before, q, part], centres[q])
                total = pltpu.roll(up, LANES - 1, 1) + pltpu.roll(down, 1, 1)
                for x in (q - 1, q + 1):
                    if 0 <= x < len(centres):
                        total = total + centres[x]
                put(p, part, total)

    def around(ring, c):
        size = ring.shape[0]
        return tuple(lax.rem(c + size + i, size) for i in (-1, 0, 1))

    def first_sum(c):
        s = slot(once, c)

        def put(p, part, total):
            once[s, p, part] = total

        neighbour_sum(cells, (c, c + 1, c + 2), [(p, p) for p in range(7)], put)

        @pl.when(jnp.logical_not(has_l))
        def _():
            clear(once, s, range(0, 2))

        @pl.when(jnp.logical_not(has_r))
        def _():
            clear(once, s, range(5, 7))

    def second_sum(c):
        s = slot(twice, c)

        def put(p, part, total):
            twice[s, p, part] = total

        neighbour_sum(once, around(once, c), [(p, p + 1) for p in range(5)], put)

        @pl.when(jnp.logical_not(has_l))
        def _():
            clear(twice, s, range(0, 1))

        @pl.when(jnp.logical_not(has_r))
        def _():
            clear(twice, s, range(4, 5))

    def third_sum(c):
        def put(p, part, total):
            columns = slice(p * LANES, (p + 1) * LANES)
            lines = pl.ds(3 * nz + part.start, ROWS)
            head[lines, columns], tail[lines, columns] = halves(total)

        neighbour_sum(twice, around(twice, c), [(p, p + 1) for p in range(3)], put)
        for k, (source, s, first) in enumerate(
            ((cells, c + 1, 2), (once, slot(once, c), 2), (twice, slot(twice, c), 1))
        ):
            lines = slice(k * nz, (k + 1) * nz)
            for p in range(3):
                columns = slice(p * LANES, (p + 1) * LANES)
                head[lines, columns], tail[lines, columns] = halves(source[s, first + p])
        product = product_of(terms, slice(0, 4 * nz), head[...], tail[...])
        for p in range(3):
            sums[slot(sums, c), p] = product[:, p * LANES : (p + 1) * LANES]

    def add_far(j):
        far = jnp.concatenate([far_l[j], far_r[j]], axis=1)
        product = product_of(terms, slice(3 * nz, 4 * nz), *halves(far))
        s = slot(sums, j)
        columns = cut(j)
        for p in range(3):
            total = sums[s, p]
            if p == 0:
                total = total + product[:, 0:LANES]
            if p == 2:
                total = total + product[:, LANES : 2 * LANES]
            sol[p, :, columns] = total[0:nz]
            for side in range(2):
                doubled[p, pl.ds(side, nz // 2, stride=2)] = total[nz:rows]
            pend[p, :, columns] = doubled[p]

    def step(c, _):
        @pl.when(c < chunks)
        def _():
            own_copy(c).wait()
            finish(near_left, near_right, c)

        @pl.when(c + AHEAD < chunks)
        def _():
            start(near_left, near_right, c + AHEAD)

            @pl.when(c + AHEAD >= LAG)
            def _():
                start(far_left, far_right, c + AHEAD - LAG)

        @pl.when(c + AHEAD == chunks)
        def _():
            for i in range(LAG):
                start(far_left, far_right, chunks - LAG + i)

        @pl.when((c >= 1) & (c < chunks + 1))
        def _():
            first_sum(c - 1)

        @pl.when(c == chunks + 1)
        def _():
            clear(once, slot(once, chunks), range(7))

        @pl.when((c >= 2) & (c < chunks + 2))
        def _():
            second_sum(c - 2)

        @pl.when(c == chunks + 2)
        def _():
            clear(twice, slot(twice, chunks), range(5))

        @pl.when((c >= 3) & (c < chunks + 3))
        def _():
            third_sum(c - 3)

        @pl.when(c >= LAG)
        def _():
            finish(far_left, far_right, c - LAG)
            add_far(c - LAG)

        return 0

    lax.fori_loop(0, chunks + LAG, step, 0)


def put_out(sol, pend, sol_out, pend_out, sems):
    copies = []
    for p in range(sol.shape[0]):
        copies.append(pltpu.make_async_copy(sol.at[p], sol_out.at[p], sems.at[0, p]))
        copies.append(pltpu.make_async_copy(pend.at[p], pend_out.at[p], sems.at[1, p]))
    for copy in copies:
        copy.start()
    for copy in copies:
        copy.wait()


def solution(mesh):
    count = mesh.shape["grp"]
    anywhere = pl.BlockSpec(memory_space=pl.ANY)
    vmem = pl.BlockSpec(memory_space=pltpu.VMEM)

    def per_device(right_side, fine, two, three, four):
        planes, nz, ny = right_side.shape
        chunks = ny // LANES
        rows = nz + nz // 2
        shape = (planes, nz, ny)

        def body(*refs):
            kernel(count, *refs)

        sol, pend = pl.pallas_call(
            body,
            out_shape=(pltpu.VMEM(shape, F32), pltpu.VMEM(shape, F32)),
            in_specs=[anywhere] * 5,
            out_specs=(vmem, vmem),
            scratch_shapes=[
                pltpu.VMEM((chunks + 2, planes + 4, nz, LANES), F32),
                pltpu.VMEM((chunks, nz, LANES), F32),
                pltpu.VMEM((chunks, nz, LANES), F32),
                pltpu.VMEM((3, planes + 4, nz, LANES), F32),
                pltpu.VMEM((3, planes + 2, nz, LANES), F32),
                pltpu.VMEM((4 * nz, planes * LANES), BF16),
                pltpu.VMEM((4 * nz, planes * LANES), BF16),
                pltpu.VMEM((LAG - 2, planes, rows, LANES), F32),
                pltpu.VMEM(fine.shape[1:], F32),
                pltpu.VMEM(two.shape, F32),
                pltpu.VMEM(three.shape, F32),
                pltpu.VMEM(four.shape, F32),
                pltpu.VMEM((3 * nz, nz), F32),
                pltpu.VMEM((3, nz, nz), F32),
                pltpu.VMEM((3 * nz, nz), F32),
                pltpu.VMEM((4, rows, nz), F32),
                pltpu.VMEM((2 * rows, 4 * nz), BF16),
                pltpu.VMEM((planes, nz, LANES), F32),
                pltpu.VMEM((2, nz // 2, nz // 2), F32),
                pltpu.VMEM((nz, nz // 2), F32),
                pltpu.SemaphoreType.DMA((chunks,)),
                pltpu.SemaphoreType.DMA((4,)),
                pltpu.SemaphoreType.DMA((2, chunks)),
                pltpu.SemaphoreType.DMA((2, chunks)),
                pltpu.SemaphoreType.DMA((2, chunks)),
                pltpu.SemaphoreType.DMA((2, chunks)),
            ],
            compiler_params=pltpu.CompilerParams(
                collective_id=1, has_side_effects=True, vmem_limit_bytes=50 << 20
            ),
        )(right_side, fine, two, three, four)
        sol = pltpu.with_memory_space_constraint(sol, pltpu.VMEM)
        pend = pltpu.with_memory_space_constraint(pend, pltpu.VMEM)
        return pl.pallas_call(
            put_out,
            out_shape=(jax.ShapeDtypeStruct(shape, F32), jax.ShapeDtypeStruct(shape, F32)),
            in_specs=[vmem, vmem],
            out_specs=(anywhere, anywhere),
            scratch_shapes=[pltpu.SemaphoreType.DMA((2, planes))],
            compiler_params=pltpu.CompilerParams(vmem_limit_bytes=16 << 20),
        )(sol, pend)

    in_specs = (P("grp", None, None), P(), P(), P(), P())
    out_specs = (P("grp", None, None), P("grp", None, None))
    return jax.shard_map(
        per_device, mesh=mesh, in_specs=in_specs, out_specs=out_specs, check_vma=False
    )
```

```python
import jax
import jax.numpy as jnp
from jax import lax
from jax.experimental import pallas as pl
from jax.experimental.pallas import tpu as pltpu
from jax.sharding import PartitionSpec as P

MESH = pl.DeviceIdType.MESH
F32 = jnp.float32
BF16 = jnp.bfloat16

FINE_Z = 4.0
LANES = 128
AHEAD = 6
LAG = 12
ROWS = 32


def parts_of(m):
    head = m.astype(BF16)
    rest = m - head.astype(F32)
    middle = rest.astype(BF16)
    return head, middle, (rest - middle.astype(F32)).astype(BF16)


def exact_dot(a, b):
    a1, a2, a3 = parts_of(a)
    b1, b2, b3 = parts_of(b)
    left = jnp.concatenate([a1, a1, a2, a1, a2, a3], axis=1)
    right = jnp.concatenate([b1, b2, b1, b3, b2, b1], axis=0)
    return jnp.dot(left, right, preferred_element_type=F32)


def second_difference(m):
    order = m.shape[0]
    row = lax.broadcasted_iota(jnp.int32, m.shape, 0)
    below = jnp.where(row == 0, 0.0, pltpu.roll(m, 1, 0))
    above = jnp.where(row == order - 1, 0.0, pltpu.roll(m, order - 1, 0))
    return 2.0 * m - below - above


def line_pair(m, vertical):
    square = exact_dot(m, m)
    mixed = exact_dot(m, second_difference(m))
    return 2.0 * m - vertical * mixed - 4.0 * square, square


def spread(rows, columns, factor):
    row = lax.broadcasted_iota(jnp.int32, (rows, columns), 0)
    column = lax.broadcasted_iota(jnp.int32, (rows, columns), 1)
    return ((row >= factor * column) & (row < factor * column + factor)).astype(F32)


def gather(rows, columns, factor):
    row = lax.broadcasted_iota(jnp.int32, (rows, columns), 0)
    column = lax.broadcasted_iota(jnp.int32, (rows, columns), 1)
    return ((column >= factor * row) & (column < factor * row + factor)).astype(F32)


def build_terms(fine, two, three, four, coarse, left_terms, right_terms, product, totals, doubled, terms):
    nz = fine.shape[0]
    half = nz // 2
    p0, q = line_pair(fine, FINE_Z)

    def scaled(m):
        return 4.0 * m + FINE_Z * second_difference(m)

    row = lax.broadcasted_iota(jnp.int32, (nz, nz), 0)
    column = lax.broadcasted_iota(jnp.int32, (nz, nz), 1)
    left_terms[0:nz] = p0
    left_terms[nz : 2 * nz] = q
    right_terms[0] = (row == column).astype(F32) - scaled(p0)
    right_terms[1] = p0 - scaled(q)
    right_terms[2] = q

    c0, c1 = line_pair(two, FINE_Z / 4.0)
    for m, factor, vertical in ((three, 2, FINE_Z / 16.0), (four, 4, FINE_Z / 64.0)):
        up, down = spread(half, half, factor), gather(half, half, factor)
        wide = exact_dot(up, jnp.concatenate(line_pair(m, vertical), axis=1))
        coarse[0:half] = wide[:, 0:half]
        coarse[half:nz] = wide[:, half:nz]
        both = exact_dot(coarse[...], down)
        c0 = c0 + both[0:half]
        c1 = c1 + both[half:nz]
    coarse[0:half] = c0
    coarse[half:nz] = c1
    both = exact_dot(coarse[...], gather(half, nz, 2))
    left_terms[2 * nz : 3 * nz] = both
    for k, base in ((0, p0), (1, q)):
        for h in range(nz // LANES):
            columns = slice(h * LANES, (h + 1) * LANES)
            part = left_terms[2 * nz + k * half : 2 * nz + (k + 1) * half, columns]
            for side in range(2):
                doubled[h, pl.ds(side, half, stride=2)] = part
            totals[k, 0:nz, columns] = base[:, columns] + doubled[h]
    for k in range(4):
        if k >= 2:
            totals[k, 0:nz] = jnp.zeros((nz, nz), F32)
        totals[k, nz : nz + half] = jnp.zeros((half, nz), F32)
    for j in range(3):
        product[...] = exact_dot(left_terms[...], right_terms[j])
        totals[j, 0:nz] += product[0:nz]
        totals[j + 1, 0:nz] += product[nz : 2 * nz]
        totals[j, nz : nz + half] += product[2 * nz : 2 * nz + half]
        totals[j + 1, nz : nz + half] += product[2 * nz + half : 3 * nz]
    for k in range(4):
        total = totals[k]
        columns = slice(k * nz, (k + 1) * nz)
        head = total.astype(BF16)
        terms[0 : nz + half, columns] = head
        terms[nz + half :, columns] = (total - head.astype(F32)).astype(BF16)


def halves(cells):
    head = cells.astype(BF16)
    return head, (cells - head.astype(F32)).astype(BF16)


def product_of(terms, columns, head, tail):
    rows = terms.shape[0] // 2
    both = jnp.dot(terms[:, columns], head, preferred_element_type=F32)
    rest = jnp.dot(terms[0:rows, columns], tail, preferred_element_type=F32)
    return both[0:rows] + (both[rows:] + rest)


def kernel(
    count,
    right_side, fine, two, three, four,
    sol, pend,
    cells, far_l, far_r,
    once, twice, head, tail, sums,
    fine_v, two_v, three_v, four_v, left_terms, right_terms, product, totals, terms, doubled, padded, coarse,
    own_sem, small_sem, near_send, near_recv, far_send, far_recv,
):
    me = lax.axis_index("grp")
    has_l, has_r = me > 0, me < count - 1
    chunks = far_l.shape[0]
    rows = sums.shape[2]
    nz = cells.shape[2]

    barrier = pltpu.get_barrier_semaphore()

    @pl.when(has_l)
    def _():
        pl.semaphore_signal(barrier, inc=1, device_id=(me - 1,), device_id_type=MESH)

    @pl.when(has_r)
    def _():
        pl.semaphore_signal(barrier, inc=1, device_id=(me + 1,), device_id_type=MESH)

    pl.semaphore_wait(barrier, has_l.astype(jnp.int32) + has_r.astype(jnp.int32))

    def cut(c):
        return pl.ds(pl.multiple_of(c * LANES, LANES), LANES)

    def remote(planes, target, sends, recvs, way, c, device):
        return pltpu.make_async_remote_copy(
            src_ref=right_side.at[planes, :, cut(c)],
            dst_ref=target,
            send_sem=sends.at[way, c],
            recv_sem=recvs.at[way, c],
            device_id=(device,),
            device_id_type=MESH,
        )

    def near_left(c):
        target = cells.at[c + 1, pl.ds(5, 2)]
        return remote(pl.ds(0, 2), target, near_send, near_recv, 0, c, me - 1)

    def near_right(c):
        target = cells.at[c + 1, pl.ds(0, 2)]
        return remote(pl.ds(1, 2), target, near_send, near_recv, 1, c, me + 1)

    def far_left(c):
        return remote(2, far_r.at[c], far_send, far_recv, 0, c, me - 1)

    def far_right(c):
        return remote(0, far_l.at[c], far_send, far_recv, 1, c, me + 1)

    def start(to_left, to_right, c):
        @pl.when(has_l)
        def _():
            to_left(c).start()

        @pl.when(has_r)
        def _():
            to_right(c).start()

    def finish(to_left, to_right, c):
        @pl.when(has_l)
        def _():
            to_left(c).wait_send()
            to_right(c).wait_recv()

        @pl.when(has_r)
        def _():
            to_right(c).wait_send()
            to_left(c).wait_recv()

    for c in range(AHEAD):
        start(near_left, near_right, c)

    small = [
        pltpu.make_async_copy(src, dst, small_sem.at[i])
        for i, (src, dst) in enumerate(
            ((fine.at[0], fine_v), (two, two_v), (three, three_v), (four, four_v))
        )
    ]
    for copy in small:
        copy.start()

    def own_copy(c):
        return pltpu.make_async_copy(
            right_side.at[:, :, cut(c)], cells.at[c + 1, pl.ds(2, 3)], own_sem.at[c]
        )

    lax.fori_loop(0, chunks, lambda c, _: (own_copy(c).start(), 0)[1], 0)

    plane = jnp.zeros((nz, LANES), F32)
    for p in range(7):
        cells[0, p] = plane
        cells[chunks + 1, p] = plane

    def clear(ring, s, planes):
        for p in planes:
            ring[s, p] = plane

    clear(once, once.shape[0] - 1, range(7))
    clear(twice, twice.shape[0] - 1, range(5))

    @pl.when(jnp.logical_not(has_l))
    def _():
        def body(c, _):
            clear(cells, c + 1, range(0, 2))
            far_l[c] = plane
            return 0

        lax.fori_loop(0, chunks, body, 0)

    @pl.when(jnp.logical_not(has_r))
    def _():
        def body(c, _):
            clear(cells, c + 1, range(5, 7))
            far_r[c] = plane
            return 0

        lax.fori_loop(0, chunks, body, 0)

    for copy in small:
        copy.wait()
    for i, m in enumerate((three_v, four_v)):
        order = m.shape[0]
        padded[i] = jnp.zeros(padded.shape[1:], F32)
        padded[i, 0:order, 0:order] = m[...]
    build_terms(fine_v[...], two_v[...], padded[0], padded[1], coarse,
        left_terms, right_terms, product, totals, doubled, terms)

    def slot(ring, c):
        return lax.rem(c, ring.shape[0])

    lane = lax.broadcasted_iota(jnp.int32, (ROWS, LANES), 1)
    first_lane, last_lane = lane == 0, lane == LANES - 1

    def neighbour_sum(source, slots, targets, put):
        before, here, after = slots
        for b in range(nz // ROWS):
            part = pl.ds(b * ROWS, ROWS)
            centres = [source[here, q, part] for q in range(source.shape[1])]
            for p, q in targets:
                up = jnp.where(first_lane, source[after, q, part], centres[q])
                down = jnp.where(last_lane, source[before, q, part], centres[q])
                total = pltpu.roll(up, LANES - 1, 1) + pltpu.roll(down, 1, 1)
                for x in (q - 1, q + 1):
                    if 0 <= x < len(centres):
                        total = total + centres[x]
                put(p, part, total)

    def around(ring, c):
        size = ring.shape[0]
        return tuple(lax.rem(c + size + i, size) for i in (-1, 0, 1))

    def first_sum(c):
        s = slot(once, c)

        def put(p, part, total):
            once[s, p, part] = total

        neighbour_sum(cells, (c, c + 1, c + 2), [(p, p) for p in range(7)], put)

        @pl.when(jnp.logical_not(has_l))
        def _():
            clear(once, s, range(0, 2))

        @pl.when(jnp.logical_not(has_r))
        def _():
            clear(once, s, range(5, 7))

    def second_sum(c):
        s = slot(twice, c)

        def put(p, part, total):
            twice[s, p, part] = total

        neighbour_sum(once, around(once, c), [(p, p + 1) for p in range(5)], put)

        @pl.when(jnp.logical_not(has_l))
        def _():
            clear(twice, s, range(0, 1))

        @pl.when(jnp.logical_not(has_r))
        def _():
            clear(twice, s, range(4, 5))

    def third_sum(c):
        def put(p, part, total):
            columns = slice(p * LANES, (p + 1) * LANES)
            lines = pl.ds(3 * nz + part.start, ROWS)
            head[lines, columns], tail[lines, columns] = halves(total)

        neighbour_sum(twice, around(twice, c), [(p, p + 1) for p in range(3)], put)
        for k, (source, s, first) in enumerate(
            ((cells, c + 1, 2), (once, slot(once, c), 2), (twice, slot(twice, c), 1))
        ):
            lines = slice(k * nz, (k + 1) * nz)
            for p in range(3):
                columns = slice(p * LANES, (p + 1) * LANES)
                head[lines, columns], tail[lines, columns] = halves(source[s, first + p])
        product = product_of(terms, slice(0, 4 * nz), head[...], tail[...])
        for p in range(3):
            sums[slot(sums, c), p] = product[:, p * LANES : (p + 1) * LANES]

    def add_far(j):
        far = jnp.concatenate([far_l[j], far_r[j]], axis=1)
        product = product_of(terms, slice(3 * nz, 4 * nz), *halves(far))
        s = slot(sums, j)
        columns = cut(j)
        for p in range(3):
            total = sums[s, p]
            if p == 0:
                total = total + product[:, 0:LANES]
            if p == 2:
                total = total + product[:, LANES : 2 * LANES]
            sol[p, :, columns] = total[0:nz]
            for side in range(2):
                doubled[p, pl.ds(side, nz // 2, stride=2)] = total[nz:rows]
            pend[p, :, columns] = doubled[p]

    def step(c, _):
        @pl.when(c < chunks)
        def _():
            own_copy(c).wait()
            finish(near_left, near_right, c)

        @pl.when(c + AHEAD < chunks)
        def _():
            start(near_left, near_right, c + AHEAD)

            @pl.when(c + AHEAD >= LAG)
            def _():
                start(far_left, far_right, c + AHEAD - LAG)

        @pl.when(c + AHEAD == chunks)
        def _():
            for i in range(LAG):
                start(far_left, far_right, chunks - LAG + i)

        @pl.when((c >= 1) & (c < chunks + 1))
        def _():
            first_sum(c - 1)

        @pl.when(c == chunks + 1)
        def _():
            clear(once, slot(once, chunks), range(7))

        @pl.when((c >= 2) & (c < chunks + 2))
        def _():
            second_sum(c - 2)

        @pl.when(c == chunks + 2)
        def _():
            clear(twice, slot(twice, chunks), range(5))

        @pl.when((c >= 3) & (c < chunks + 3))
        def _():
            third_sum(c - 3)

        @pl.when(c >= LAG)
        def _():
            finish(far_left, far_right, c - LAG)
            add_far(c - LAG)

        return 0

    lax.fori_loop(0, chunks + LAG, step, 0)


def put_out(sol, pend, sol_out, pend_out, sems):
    copies = []
    for p in range(sol.shape[0]):
        copies.append(pltpu.make_async_copy(sol.at[p], sol_out.at[p], sems.at[0, p]))
        copies.append(pltpu.make_async_copy(pend.at[p], pend_out.at[p], sems.at[1, p]))
    for copy in copies:
        copy.start()
    for copy in copies:
        copy.wait()


def solution(mesh):
    count = mesh.shape["grp"]
    anywhere = pl.BlockSpec(memory_space=pl.ANY)
    vmem = pl.BlockSpec(memory_space=pltpu.VMEM)

    def per_device(right_side, fine, two, three, four):
        planes, nz, ny = right_side.shape
        chunks = ny // LANES
        rows = nz + nz // 2
        shape = (planes, nz, ny)

        def body(*refs):
            kernel(count, *refs)

        sol, pend = pl.pallas_call(
            body,
            out_shape=(pltpu.VMEM(shape, F32), pltpu.VMEM(shape, F32)),
            in_specs=[anywhere] * 5,
            out_specs=(vmem, vmem),
            scratch_shapes=[
                pltpu.VMEM((chunks + 2, planes + 4, nz, LANES), F32),
                pltpu.VMEM((chunks, nz, LANES), F32),
                pltpu.VMEM((chunks, nz, LANES), F32),
                pltpu.VMEM((3, planes + 4, nz, LANES), F32),
                pltpu.VMEM((3, planes + 2, nz, LANES), F32),
                pltpu.VMEM((4 * nz, planes * LANES), BF16),
                pltpu.VMEM((4 * nz, planes * LANES), BF16),
                pltpu.VMEM((LAG - 2, planes, rows, LANES), F32),
                pltpu.VMEM(fine.shape[1:], F32),
                pltpu.VMEM(two.shape, F32),
                pltpu.VMEM(three.shape, F32),
                pltpu.VMEM(four.shape, F32),
                pltpu.VMEM((3 * nz, nz), F32),
                pltpu.VMEM((3, nz, nz), F32),
                pltpu.VMEM((3 * nz, nz), F32),
                pltpu.VMEM((4, rows, nz), F32),
                pltpu.VMEM((2 * rows, 4 * nz), BF16),
                pltpu.VMEM((planes, nz, LANES), F32),
                pltpu.VMEM((2, nz // 2, nz // 2), F32),
                pltpu.VMEM((nz, nz // 2), F32),
                pltpu.SemaphoreType.DMA((chunks,)),
                pltpu.SemaphoreType.DMA((4,)),
                pltpu.SemaphoreType.DMA((2, chunks)),
                pltpu.SemaphoreType.DMA((2, chunks)),
                pltpu.SemaphoreType.DMA((2, chunks)),
                pltpu.SemaphoreType.DMA((2, chunks)),
            ],
            compiler_params=pltpu.CompilerParams(
                collective_id=1, has_side_effects=True, vmem_limit_bytes=50 << 20
            ),
        )(right_side, fine, two, three, four)
        sol = pltpu.with_memory_space_constraint(sol, pltpu.VMEM)
        pend = pltpu.with_memory_space_constraint(pend, pltpu.VMEM)
        return pl.pallas_call(
            put_out,
            out_shape=(jax.ShapeDtypeStruct(shape, F32), jax.ShapeDtypeStruct(shape, F32)),
            in_specs=[vmem, vmem],
            out_specs=(anywhere, anywhere),
            scratch_shapes=[pltpu.SemaphoreType.DMA((2, planes))],
            compiler_params=pltpu.CompilerParams(vmem_limit_bytes=16 << 20),
        )(sol, pend)

    in_specs = (P("grp", None, None), P(), P(), P(), P())
    out_specs = (P("grp", None, None), P("grp", None, None))
    return jax.shard_map(
        per_device, mesh=mesh, in_specs=in_specs, out_specs=out_specs, check_vma=False
    )
```

```python
import jax
import jax.numpy as jnp
from jax import lax
from jax.experimental import pallas as pl
from jax.experimental.pallas import tpu as pltpu
from jax.sharding import PartitionSpec as P

MESH = pl.DeviceIdType.MESH
F32 = jnp.float32
BF16 = jnp.bfloat16

FINE_Z = 4.0
LANES = 128
AHEAD = 6
LAG = 12
ROWS = 32


def parts_of(m):
    head = m.astype(BF16)
    rest = m - head.astype(F32)
    middle = rest.astype(BF16)
    return head, middle, (rest - middle.astype(F32)).astype(BF16)


def exact_dot(a, b):
    a1, a2, a3 = parts_of(a)
    b1, b2, b3 = parts_of(b)
    left = jnp.concatenate([a1, a1, a2, a1, a2, a3], axis=1)
    right = jnp.concatenate([b1, b2, b1, b3, b2, b1], axis=0)
    return jnp.dot(left, right, preferred_element_type=F32)


def second_difference(m):
    order = m.shape[0]
    row = lax.broadcasted_iota(jnp.int32, m.shape, 0)
    below = jnp.where(row == 0, 0.0, pltpu.roll(m, 1, 0))
    above = jnp.where(row == order - 1, 0.0, pltpu.roll(m, order - 1, 0))
    return 2.0 * m - below - above


def line_pair(m, vertical):
    square = exact_dot(m, m)
    mixed = exact_dot(m, second_difference(m))
    return 2.0 * m - vertical * mixed - 4.0 * square, square


def spread(rows, columns, factor):
    row = lax.broadcasted_iota(jnp.int32, (rows, columns), 0)
    column = lax.broadcasted_iota(jnp.int32, (rows, columns), 1)
    return ((row >= factor * column) & (row < factor * column + factor)).astype(F32)


def gather(rows, columns, factor):
    row = lax.broadcasted_iota(jnp.int32, (rows, columns), 0)
    column = lax.broadcasted_iota(jnp.int32, (rows, columns), 1)
    return ((column >= factor * row) & (column < factor * row + factor)).astype(F32)


def build_terms(fine, two, three, four, coarse, left_terms, right_terms, product, totals, doubled, terms):
    nz = fine.shape[0]
    half = nz // 2
    p0, q = line_pair(fine, FINE_Z)

    def scaled(m):
        return 4.0 * m + FINE_Z * second_difference(m)

    row = lax.broadcasted_iota(jnp.int32, (nz, nz), 0)
    column = lax.broadcasted_iota(jnp.int32, (nz, nz), 1)
    left_terms[0:nz] = p0
    left_terms[nz : 2 * nz] = q
    right_terms[0] = (row == column).astype(F32) - scaled(p0)
    right_terms[1] = p0 - scaled(q)
    right_terms[2] = q

    c0, c1 = line_pair(two, FINE_Z / 4.0)
    for m, factor, vertical in ((three, 2, FINE_Z / 16.0), (four, 4, FINE_Z / 64.0)):
        up, down = spread(half, half, factor), gather(half, half, factor)
        wide = exact_dot(up, jnp.concatenate(line_pair(m, vertical), axis=1))
        coarse[0:half] = wide[:, 0:half]
        coarse[half:nz] = wide[:, half:nz]
        both = exact_dot(coarse[...], down)
        c0 = c0 + both[0:half]
        c1 = c1 + both[half:nz]
    coarse[0:half] = c0
    coarse[half:nz] = c1
    both = exact_dot(coarse[...], gather(half, nz, 2))
    left_terms[2 * nz : 3 * nz] = both
    for k, base in ((0, p0), (1, q)):
        for h in range(nz // LANES):
            columns = slice(h * LANES, (h + 1) * LANES)
            part = left_terms[2 * nz + k * half : 2 * nz + (k + 1) * half, columns]
            for side in range(2):
                doubled[h, pl.ds(side, half, stride=2)] = part
            totals[k, 0:nz, columns] = base[:, columns] + doubled[h]
    for k in range(4):
        if k >= 2:
            totals[k, 0:nz] = jnp.zeros((nz, nz), F32)
        totals[k, nz : nz + half] = jnp.zeros((half, nz), F32)
    for j in range(3):
        product[...] = exact_dot(left_terms[...], right_terms[j])
        totals[j, 0:nz] += product[0:nz]
        totals[j + 1, 0:nz] += product[nz : 2 * nz]
        totals[j, nz : nz + half] += product[2 * nz : 2 * nz + half]
        totals[j + 1, nz : nz + half] += product[2 * nz + half : 3 * nz]
    for k in range(4):
        total = totals[k]
        columns = slice(k * nz, (k + 1) * nz)
        head = total.astype(BF16)
        terms[0 : nz + half, columns] = head
        terms[nz + half :, columns] = (total - head.astype(F32)).astype(BF16)


def halves(cells):
    head = cells.astype(BF16)
    return head, (cells - head.astype(F32)).astype(BF16)


def product_of(terms, columns, head, tail):
    rows = terms.shape[0] // 2
    both = jnp.dot(terms[:, columns], head, preferred_element_type=F32)
    rest = jnp.dot(terms[0:rows, columns], tail, preferred_element_type=F32)
    return both[0:rows] + (both[rows:] + rest)


def kernel(
    count,
    right_side, fine, two, three, four,
    sol, pend,
    cells, far_l, far_r,
    once, twice, head, tail, sums,
    fine_v, two_v, three_v, four_v, left_terms, right_terms, product, totals, terms, doubled, padded, coarse,
    own_sem, small_sem, near_send, near_recv, far_send, far_recv,
):
    me = lax.axis_index("grp")
    has_l, has_r = me > 0, me < count - 1
    chunks = far_l.shape[0]
    rows = sums.shape[2]
    nz = cells.shape[2]

    barrier = pltpu.get_barrier_semaphore()

    @pl.when(has_l)
    def _():
        pl.semaphore_signal(barrier, inc=1, device_id=(me - 1,), device_id_type=MESH)

    @pl.when(has_r)
    def _():
        pl.semaphore_signal(barrier, inc=1, device_id=(me + 1,), device_id_type=MESH)

    pl.semaphore_wait(barrier, has_l.astype(jnp.int32) + has_r.astype(jnp.int32))

    def cut(c, lanes=LANES):
        return pl.ds(pl.multiple_of(c * lanes, lanes), lanes)

    def remote(planes, target, sends, recvs, way, c, device, lanes=LANES):
        return pltpu.make_async_remote_copy(
            src_ref=right_side.at[planes, :, cut(c, lanes)],
            dst_ref=target,
            send_sem=sends.at[way, c],
            recv_sem=recvs.at[way, c],
            device_id=(device,),
            device_id_type=MESH,
        )

    def near_left(u):
        target = cells.at[u + 1, pl.ds(5, 2)]
        return remote(pl.ds(0, 2), target, near_send, near_recv, 0, u, me - 1, 2 * LANES)

    def near_right(u):
        target = cells.at[u + 1, pl.ds(0, 2)]
        return remote(pl.ds(1, 2), target, near_send, near_recv, 1, u, me + 1, 2 * LANES)

    def far_left(c):
        return remote(2, far_r.at[c], far_send, far_recv, 0, c, me - 1)

    def far_right(c):
        return remote(0, far_l.at[c], far_send, far_recv, 1, c, me + 1)

    def start(to_left, to_right, c):
        @pl.when(has_l)
        def _():
            to_left(c).start()

        @pl.when(has_r)
        def _():
            to_right(c).start()

    def finish(to_left, to_right, c):
        @pl.when(has_l)
        def _():
            to_left(c).wait_send()
            to_right(c).wait_recv()

        @pl.when(has_r)
        def _():
            to_right(c).wait_send()
            to_left(c).wait_recv()

    for u in range(AHEAD // 2):
        start(near_left, near_right, u)

    small = [
        pltpu.make_async_copy(src, dst, small_sem.at[i])
        for i, (src, dst) in enumerate(
            ((fine.at[0], fine_v), (two, two_v), (three, three_v), (four, four_v))
        )
    ]
    for copy in small:
        copy.start()

    def own_copy(u):
        return pltpu.make_async_copy(
            right_side.at[:, :, cut(u, 2 * LANES)], cells.at[u + 1, pl.ds(2, 3)], own_sem.at[u]
        )

    lax.fori_loop(0, chunks // 2, lambda u, _: (own_copy(u).start(), 0)[1], 0)

    plane = jnp.zeros((nz, LANES), F32)
    for p in range(7):
        cells[0, p, :, LANES:] = plane
        cells[chunks // 2 + 1, p, :, 0:LANES] = plane

    def clear(ring, s, planes):
        for p in planes:
            ring[s, p] = plane

    clear(once, once.shape[0] - 1, range(7))
    clear(twice, twice.shape[0] - 1, range(5))

    @pl.when(jnp.logical_not(has_l))
    def _():
        def body(c, _):
            for p in range(0, 2):
                cells[1 + c // 2, p, :, cut(lax.rem(c, 2))] = plane
            far_l[c] = plane
            return 0

        lax.fori_loop(0, chunks, body, 0)

    @pl.when(jnp.logical_not(has_r))
    def _():
        def body(c, _):
            for p in range(5, 7):
                cells[1 + c // 2, p, :, cut(lax.rem(c, 2))] = plane
            far_r[c] = plane
            return 0

        lax.fori_loop(0, chunks, body, 0)

    for copy in small:
        copy.wait()
    for i, m in enumerate((three_v, four_v)):
        order = m.shape[0]
        padded[i] = jnp.zeros(padded.shape[1:], F32)
        padded[i, 0:order, 0:order] = m[...]
    build_terms(fine_v[...], two_v[...], padded[0], padded[1], coarse,
        left_terms, right_terms, product, totals, doubled, terms)

    def slot(ring, c):
        return lax.rem(c, ring.shape[0])

    lane = lax.broadcasted_iota(jnp.int32, (ROWS, LANES), 1)
    first_lane, last_lane = lane == 0, lane == LANES - 1

    def neighbour_sum(count_of, views, targets, put):
        before, here, after = views
        for b in range(nz // ROWS):
            part = pl.ds(b * ROWS, ROWS)
            centres = [here(q, part) for q in range(count_of)]
            for p, q in targets:
                up = jnp.where(first_lane, after(q, part), centres[q])
                down = jnp.where(last_lane, before(q, part), centres[q])
                total = pltpu.roll(up, LANES - 1, 1) + pltpu.roll(down, 1, 1)
                for x in (q - 1, q + 1):
                    if 0 <= x < len(centres):
                        total = total + centres[x]
                put(p, part, total)

    def around(ring, c):
        size = ring.shape[0]
        slots = [lax.rem(c + size + i, size) for i in (-1, 0, 1)]
        return [lambda q, part, s=s: ring[s, q, part] for s in slots]

    def cells_at(c):
        u, columns = lax.div(c + 2, 2), cut(lax.rem(c + 2, 2))
        return lambda q, part: cells[u, q, part, columns]

    def first_sum(c):
        s = slot(once, c)

        def put(p, part, total):
            once[s, p, part] = total

        neighbour_sum(7, [cells_at(c + i) for i in (-1, 0, 1)], [(p, p) for p in range(7)], put)

        @pl.when(jnp.logical_not(has_l))
        def _():
            clear(once, s, range(0, 2))

        @pl.when(jnp.logical_not(has_r))
        def _():
            clear(once, s, range(5, 7))

    def second_sum(c):
        s = slot(twice, c)

        def put(p, part, total):
            twice[s, p, part] = total

        neighbour_sum(7, around(once, c), [(p, p + 1) for p in range(5)], put)

        @pl.when(jnp.logical_not(has_l))
        def _():
            clear(twice, s, range(0, 1))

        @pl.when(jnp.logical_not(has_r))
        def _():
            clear(twice, s, range(4, 5))

    def third_sum(c):
        def put(p, part, total):
            columns = slice(p * LANES, (p + 1) * LANES)
            lines = pl.ds(3 * nz + part.start, ROWS)
            head[lines, columns], tail[lines, columns] = halves(total)

        neighbour_sum(5, around(twice, c), [(p, p + 1) for p in range(3)], put)
        views = ((cells_at(c), 2), (around(once, c)[1], 2), (around(twice, c)[1], 1))
        for k, (view, first) in enumerate(views):
            lines = slice(k * nz, (k + 1) * nz)
            for p in range(3):
                columns = slice(p * LANES, (p + 1) * LANES)
                head[lines, columns], tail[lines, columns] = halves(view(first + p, pl.ds(0, nz)))
        product = product_of(terms, slice(0, 4 * nz), head[...], tail[...])
        for p in range(3):
            sums[slot(sums, c), p] = product[:, p * LANES : (p + 1) * LANES]

    def add_far(j):
        far = jnp.concatenate([far_l[j], far_r[j]], axis=1)
        product = product_of(terms, slice(3 * nz, 4 * nz), *halves(far))
        s = slot(sums, j)
        columns = cut(j)
        for p in range(3):
            total = sums[s, p]
            if p == 0:
                total = total + product[:, 0:LANES]
            if p == 2:
                total = total + product[:, LANES : 2 * LANES]
            sol[p, :, columns] = total[0:nz]
            for side in range(2):
                doubled[p, pl.ds(side, nz // 2, stride=2)] = total[nz:rows]
            pend[p, :, columns] = doubled[p]

    def step(c, _):
        pair = lax.div(c, 2)
        is_even = lax.rem(c, 2) == 0

        @pl.when(is_even & (c < chunks))
        def _():
            own_copy(pair).wait()
            finish(near_left, near_right, pair)

        @pl.when(is_even & (c + AHEAD < chunks))
        def _():
            start(near_left, near_right, pair + AHEAD // 2)

        @pl.when((c + AHEAD < chunks) & (c + AHEAD >= LAG))
        def _():
            start(far_left, far_right, c + AHEAD - LAG)

        @pl.when(c + AHEAD == chunks)
        def _():
            for i in range(LAG):
                start(far_left, far_right, chunks - LAG + i)

        @pl.when((c >= 1) & (c < chunks + 1))
        def _():
            first_sum(c - 1)

        @pl.when(c == chunks + 1)
        def _():
            clear(once, slot(once, chunks), range(7))

        @pl.when((c >= 2) & (c < chunks + 2))
        def _():
            second_sum(c - 2)

        @pl.when(c == chunks + 2)
        def _():
            clear(twice, slot(twice, chunks), range(5))

        @pl.when((c >= 3) & (c < chunks + 3))
        def _():
            third_sum(c - 3)

        @pl.when(c >= LAG)
        def _():
            finish(far_left, far_right, c - LAG)
            add_far(c - LAG)

        return 0

    lax.fori_loop(0, chunks + LAG, step, 0)


def put_out(sol, pend, sol_out, pend_out, sems):
    copies = []
    for p in range(sol.shape[0]):
        copies.append(pltpu.make_async_copy(sol.at[p], sol_out.at[p], sems.at[0, p]))
        copies.append(pltpu.make_async_copy(pend.at[p], pend_out.at[p], sems.at[1, p]))
    for copy in copies:
        copy.start()
    for copy in copies:
        copy.wait()


def solution(mesh):
    count = mesh.shape["grp"]
    anywhere = pl.BlockSpec(memory_space=pl.ANY)
    vmem = pl.BlockSpec(memory_space=pltpu.VMEM)

    def per_device(right_side, fine, two, three, four):
        planes, nz, ny = right_side.shape
        chunks = ny // LANES
        rows = nz + nz // 2
        shape = (planes, nz, ny)

        def body(*refs):
            kernel(count, *refs)

        sol, pend = pl.pallas_call(
            body,
            out_shape=(pltpu.VMEM(shape, F32), pltpu.VMEM(shape, F32)),
            in_specs=[anywhere] * 5,
            out_specs=(vmem, vmem),
            scratch_shapes=[
                pltpu.VMEM((chunks // 2 + 2, planes + 4, nz, 2 * LANES), F32),
                pltpu.VMEM((chunks, nz, LANES), F32),
                pltpu.VMEM((chunks, nz, LANES), F32),
                pltpu.VMEM((3, planes + 4, nz, LANES), F32),
                pltpu.VMEM((3, planes + 2, nz, LANES), F32),
                pltpu.VMEM((4 * nz, planes * LANES), BF16),
                pltpu.VMEM((4 * nz, planes * LANES), BF16),
                pltpu.VMEM((LAG - 2, planes, rows, LANES), F32),
                pltpu.VMEM(fine.shape[1:], F32),
                pltpu.VMEM(two.shape, F32),
                pltpu.VMEM(three.shape, F32),
                pltpu.VMEM(four.shape, F32),
                pltpu.VMEM((3 * nz, nz), F32),
                pltpu.VMEM((3, nz, nz), F32),
                pltpu.VMEM((3 * nz, nz), F32),
                pltpu.VMEM((4, rows, nz), F32),
                pltpu.VMEM((2 * rows, 4 * nz), BF16),
                pltpu.VMEM((planes, nz, LANES), F32),
                pltpu.VMEM((2, nz // 2, nz // 2), F32),
                pltpu.VMEM((nz, nz // 2), F32),
                pltpu.SemaphoreType.DMA((chunks // 2,)),
                pltpu.SemaphoreType.DMA((4,)),
                pltpu.SemaphoreType.DMA((2, chunks)),
                pltpu.SemaphoreType.DMA((2, chunks)),
                pltpu.SemaphoreType.DMA((2, chunks)),
                pltpu.SemaphoreType.DMA((2, chunks)),
            ],
            compiler_params=pltpu.CompilerParams(
                collective_id=1, has_side_effects=True, vmem_limit_bytes=50 << 20
            ),
        )(right_side, fine, two, three, four)
        sol = pltpu.with_memory_space_constraint(sol, pltpu.VMEM)
        pend = pltpu.with_memory_space_constraint(pend, pltpu.VMEM)
        return pl.pallas_call(
            put_out,
            out_shape=(jax.ShapeDtypeStruct(shape, F32), jax.ShapeDtypeStruct(shape, F32)),
            in_specs=[vmem, vmem],
            out_specs=(anywhere, anywhere),
            scratch_shapes=[pltpu.SemaphoreType.DMA((2, planes))],
            compiler_params=pltpu.CompilerParams(vmem_limit_bytes=16 << 20),
        )(sol, pend)

    in_specs = (P("grp", None, None), P(), P(), P(), P())
    out_specs = (P("grp", None, None), P("grp", None, None))
    return jax.shard_map(
        per_device, mesh=mesh, in_specs=in_specs, out_specs=out_specs, check_vma=False
    )
```
